256 devices in a mesh: dp: 32 (over y_lo, z, core), fsdp: 8 (over y_hi, x).
Axes of the slice: x: 4, y: 4 (y_hi: 2, y_lo: 2; y = y_hi * 2 + y_lo), z: 8, core: 2. Of those that a mesh axis runs over, the one named last changes fastest.
Arguments:
- activations: bfloat16 [4096, 8192], P('dp', 'fsdp'), may hold values from -6 to 6
- projector: bfloat16 [8192, 1024], P('fsdp'), may hold values from -0.0625 to 0.0625
- out_grad: bfloat16 [4096, 8, 3584], P('dp', 'fsdp'), may hold values from -0.1875 to 0.1875
- first_moment: float32 [8, 3584, 1024], P('fsdp', 'dp'), may hold values from -4 to 4
- second_moment: float32 [8, 3584, 1024], P('fsdp', 'dp'), may hold values from 0.002 to 0.05
Outputs:
- weight_update: bfloat16 [8, 3584, 8192], P(None, 'dp', 'fsdp')
- first_new: float32 [8, 3584, 1024], P('fsdp', 'dp')
- second_new: float32 [8, 3584, 1024], P('fsdp', 'dp')
The draws below stay inside these ranges and needn't reach their ends.
All inputs are finite; a program needn't handle non-finite values.
Results may differ from the reference program's by a relative error of at most 0.0051.
Values may be sent and summed in bfloat16 or wider, within the bound.
No kernel may reach another device: no remote copies, remote signals or barrier semaphores. Data moves between devices by JAX's collectives and lax.ppermute only.
A program may use at most 128 MiB of HBM per device.

```python
import math
import jax
import jax.numpy as jnp
from jax import lax

D = 8192
RANK = 1024
TOKENS = 4096
FB = 3584
N_FSDP = 8


def with_spikes(result, stream_key, source, target, shards_of, factor):
    owner, partner = [(jnp.arange(result.shape[dim]) // (result.shape[dim] // shards_of)).reshape([-1 if axis == dim else 1 for axis in range(result.ndim)]) for dim in (source, target)]
    chosen = jax.random.permutation(stream_key, shards_of)[partner]
    strong = (owner == chosen) | (owner == (partner + shards_of // 2) % shards_of)
    return jnp.where(strong, factor * result, result)


def block_levels(key, extent, pieces, low, largest):
    loudness = 1.0
    for position, shards_of in pieces:
        steps = jax.random.uniform(jax.random.fold_in(jax.random.fold_in(key, 6), position), (shards_of,), jnp.float32, low / len(pieces), largest / len(pieces))
        loudness = loudness * jnp.repeat(jnp.exp(steps), extent[position] // shards_of).reshape((-1,) + (1,) * (len(extent) - 1 - position))
    return loudness


def normal_values(stream_key, dims, spread, bound, split=(), dtype=jnp.bfloat16):
    entries = spread * jax.random.normal(stream_key, dims, jnp.float32)
    if split:
        entries = entries * block_levels(stream_key, dims, split, -0.22, 0.18)
    return jnp.clip(entries, -bound, bound).astype(dtype)


def noise_with(rng, extent, scale, limit, pieces, heavy, held_as=jnp.bfloat16):
    drawn = scale * jax.random.normal(rng, extent, jnp.float32)
    if pieces:
        drawn = drawn * block_levels(rng, extent, pieces, -0.22, 0.18)
    return jnp.clip(with_spikes(drawn, jax.random.fold_in(rng, 3), *heavy), -limit, limit).astype(held_as)


def setup_inputs(seed: int = 0) -> dict:
    keys = jax.random.split(jax.random.key(seed), 6)
    activations = normal_values(keys[0], (TOKENS, D), 1.0, 6.0, ((0, 32), (1, 8)))
    projector = normal_values(keys[1], (D, RANK), D ** -0.5, 0.0625, ((0, 8),))
    out_grad = noise_with(keys[2], (TOKENS, N_FSDP, FB), TOKENS ** -0.5, 0.1875, ((0, 32), (1, 8)), (0, 2, 32, 2.75))
    first_moment = normal_values(keys[3], (N_FSDP, FB, RANK), 0.3, 4.0, ((0, 8), (1, 32)), jnp.float32)
    second_moment = jnp.clip(jnp.exp(math.log(0.05) - 3.218876 * jax.random.uniform(keys[4], (N_FSDP, FB, RANK), jnp.float32) ** block_levels(keys[4], (N_FSDP, FB, RANK), ((0, 8), (1, 32)), -0.2, 0.2)), 0.002, 0.05)
    return dict(activations=activations, projector=projector, out_grad=out_grad, first_moment=first_moment, second_moment=second_moment)


bias_first = 1.0 - 0.9 ** 20
bias_second = 1.0 - 0.999 ** 20
epsilon = 1e-08

def reference(activations, projector, out_grad, first_moment, second_moment):
    projected = jnp.dot(activations, projector, preferred_element_type=jnp.float32).astype(jnp.bfloat16)
    flat_grad = out_grad.reshape(TOKENS, N_FSDP * FB)
    gradient = lax.dot_general(flat_grad, projected, (((0,), (0,)), ((), ())), preferred_element_type=jnp.float32)
    gradient = gradient.reshape(N_FSDP, FB, RANK)
    first_new = 0.9 * first_moment + 0.1 * gradient
    second_new = 0.999 * second_moment + 0.001 * gradient * gradient
    direction = (first_new / bias_first / (jnp.sqrt(second_new / bias_second) + epsilon)).astype(jnp.bfloat16)
    weight_update = lax.dot_general(direction, projector, (((2,), (1,)), ((), ())), preferred_element_type=jnp.float32)
    return (weight_update.astype(jnp.bfloat16), first_new, second_new)
```

```python
import jax
import jax.numpy as jnp
from jax import lax
from jax.sharding import Mesh, PartitionSpec as P

bias_first = 1.0 - 0.9**20
bias_second = 1.0 - 0.999**20
epsilon = 1e-08

YLO, ZH, ZL, CORE = 2, 4, 2, 2
DP = ("ylo", "zh", "zl", "core")


def swap(value, axis):
    return lax.ppermute(value, axis, [(0, 1), (1, 0)])


def shift(value, axis, size, step):
    return lax.ppermute(value, axis, [(i, (i + step) % size) for i in range(size)])


def half(value, axis, index):
    return lax.dynamic_index_in_dim(value, index, axis, keepdims=False)


def shards(activations, projector, out_grad, first_moment, second_moment):
    n_fsdp = lax.axis_size("fsdp")
    zh, zl, core, ylo = (lax.axis_index(a) for a in ("zh", "zl", "core", "ylo"))
    tokens, rank = activations.shape[0], projector.shape[1]
    cols = first_moment.shape[1]
    wide = jnp.float32
    narrow = jnp.bfloat16

    grads = out_grad.reshape(tokens, YLO, ZH, ZL * CORE * cols)
    kept = [half(grads, 2, zh)]
    for step in range(1, ZH):
        kept.append(shift(half(grads, 2, (zh + step) % ZH), "zh", ZH, step))
    grads = jnp.stack(kept)

    partial_value = jnp.dot(activations, projector, preferred_element_type=wide).astype(narrow)
    pieces = lax.all_to_all(partial_value.reshape(n_fsdp, tokens // n_fsdp, rank), "fsdp", 0, 0)
    piece = pieces.astype(wide).sum(0).astype(narrow)
    piece = jnp.stack([piece] + [shift(piece, "zh", ZH, step) for step in range(1, ZH)])
    projected = lax.all_to_all(jnp.broadcast_to(piece, (n_fsdp,) + piece.shape), "fsdp", 0, 0)

    grads = grads.reshape(ZH, n_fsdp, tokens // n_fsdp, YLO * ZL * CORE * cols)
    total = lax.dot_general(
        grads, projected, (((0, 1, 2), (1, 0, 2)), ((), ())), preferred_element_type=wide
    )
    total = total.reshape(YLO, ZL, CORE, cols, rank)
    total = half(total, 2, core) + swap(half(total, 2, 1 - core).astype(narrow), "core").astype(wide)
    left, right = total[..., : rank // 2], total[..., rank // 2 :]
    left_in = swap(half(left, 0, 1 - ylo).astype(narrow), "ylo")
    right_in = swap(half(right, 1, 1 - zl).astype(narrow), "zl")
    left = half(left, 0, ylo) + left_in.astype(wide)
    right = half(right, 1, zl) + right_in.astype(wide)
    left_in = swap(half(left, 0, 1 - zl).astype(narrow), "zl")
    right_in = swap(half(right, 0, 1 - ylo).astype(narrow), "ylo")
    left = half(left, 0, zl) + left_in.astype(wide)
    right = half(right, 0, ylo) + right_in.astype(wide)
    gradient = jnp.concatenate([left, right], axis=-1)[None]

    first_new = 0.9 * first_moment + 0.1 * gradient
    second_new = 0.999 * second_moment + 0.001 * gradient * gradient
    direction = (first_new / bias_first / (jnp.sqrt(second_new / bias_second) + epsilon)).astype(narrow)
    direction = lax.all_to_all(jnp.broadcast_to(direction, (n_fsdp, cols, rank)), "fsdp", 0, 0)
    weight_update = lax.dot_general(
        direction, projector, (((2,), (1,)), ((), ())), preferred_element_type=wide
    ).astype(narrow)
    return (weight_update, first_new, second_new)


def solution(mesh):
    fine = Mesh(
        mesh.devices.reshape(YLO, ZH, ZL, CORE, mesh.devices.shape[1]), DP + ("fsdp",)
    )
    in_specs = (
        P(DP, "fsdp"),
        P("fsdp", None),
        P(DP, "fsdp", None),
        P("fsdp", DP, None),
        P("fsdp", DP, None),
    )
    out_specs = (P(None, DP, "fsdp"), P("fsdp", DP, None), P("fsdp", DP, None))
    return jax.shard_map(shards, mesh=fine, in_specs=in_specs, out_specs=out_specs, check_vma=False)
```

```python
import functools

import jax
import jax.numpy as jnp
from jax import lax
from jax.experimental import pallas as pl
from jax.experimental.pallas import tpu as pltpu
from jax.sharding import Mesh, PartitionSpec as P

bias_first = 1.0 - 0.9**20
bias_second = 1.0 - 0.999**20
epsilon = 1e-08

YLO, ZH, ZL, CORE = 2, 4, 2, 2
DP = ("ylo", "zh", "zl", "core")
wide, narrow = jnp.float32, jnp.bfloat16
VMEM = pl.BlockSpec(memory_space=pltpu.VMEM)
SMEM = pl.BlockSpec(memory_space=pltpu.SMEM)


def swap(value, axis):
    return lax.ppermute(value, axis, [(0, 1), (1, 0)])


def shift(value, axis, size, step):
    return lax.ppermute(value, axis, [(i, (i + step) % size) for i in range(size)])


def local(body, outs, count, **kwargs):
    return pl.pallas_call(
        body,
        out_shape=[jax.ShapeDtypeStruct(shape, dtype) for shape, dtype in outs],
        in_specs=[SMEM] + [VMEM] * count,
        out_specs=[VMEM] * len(outs),
        compiler_params=pltpu.CompilerParams(vmem_limit_bytes=40 * 2**20),
        **kwargs,
    )


def turn_kernel(zh_ref, grads_ref, *refs):
    outs, turned = refs[:ZH], refs[ZH]
    turned[...] = grads_ref[...].T
    block = outs[0].shape[1]
    for step in range(ZH):
        owner = lax.rem(zh_ref[0] + step, ZH)
        for y in range(YLO):
            start = pl.multiple_of((y * ZH + owner) * block, 16)
            outs[step][y] = turned[pl.ds(start, block), :]


def rows_of_core(place_ref, core, grads, rows, sems):
    copies = []
    for step in range(ZH):
        for part in range(YLO * ZL):
            y = lax.rem(place_ref[0] + part % 2, YLO)
            z = lax.rem(place_ref[1] + part // 2, ZL)
            copies.append(
                pltpu.make_async_copy(
                    grads[step].at[y, z, core], rows.at[step, part], sems.at[step, part]
                )
            )
    for copy in copies:
        copy.start()
    return copies


def product(projected_ref, rows, copies):
    parts, cols, tokens = rows.shape[1:]
    acc = None
    for step in range(ZH):
        for copy in copies[step * parts : (step + 1) * parts]:
            copy.wait()
        part = jnp.dot(
            rows[step].reshape(parts * cols, tokens),
            projected_ref[:, step].reshape(tokens, projected_ref.shape[-1]),
            preferred_element_type=wide,
        )
        acc = part if acc is None else acc + part
    return acc.reshape(parts, cols, -1)


def send_kernel(place_ref, projected_ref, *refs):
    grads, (out_ref, rows, sems) = refs[:ZH], refs[ZH:]
    copies = rows_of_core(place_ref, 1 - place_ref[2], grads, rows, sems)
    out_ref[...] = product(projected_ref, rows, copies).astype(narrow)


def keep_kernel(place_ref, projected_ref, *refs):
    grads, (came_ref, own_ref, *sent_refs, rows, sems) = refs[:ZH], refs[ZH:]
    copies = rows_of_core(place_ref, place_ref[2], grads, rows, sems)
    total = product(projected_ref, rows, copies) + came_ref[...].astype(wide)
    own_ref[...] = total[0]
    for part, ref in enumerate(sent_refs):
        ref[...] = total[part + 1].astype(narrow)


def gradient_call(body, outs, tokens, cols, extra):
    parts = YLO * ZL
    return pl.pallas_call(
        body,
        out_shape=[jax.ShapeDtypeStruct(shape, dtype) for shape, dtype in outs],
        in_specs=[SMEM, VMEM] + [pl.BlockSpec(memory_space=pl.ANY)] * ZH + [VMEM] * extra,
        out_specs=[VMEM] * len(outs),
        scratch_shapes=[
            pltpu.VMEM((ZH, parts, cols, tokens), narrow),
            pltpu.SemaphoreType.DMA((ZH, parts)),
        ],
        compiler_params=pltpu.CompilerParams(vmem_limit_bytes=40 * 2**20),
    )


def shards(activations, projector, out_grad, first_moment, second_moment):
    n_fsdp = lax.axis_size("fsdp")
    zh, zl, core, ylo = (lax.axis_index(a) for a in ("zh", "zl", "core", "ylo"))
    tokens, rank = activations.shape[0], projector.shape[1]
    cols = first_moment.shape[1]
    block = ZL * CORE * cols

    partial_value = jnp.dot(activations, projector, preferred_element_type=wide).astype(narrow)
    partial_value, out_grad = lax.optimization_barrier((partial_value, out_grad))
    pieces = lax.all_to_all(partial_value.reshape(n_fsdp, tokens // n_fsdp, rank), "fsdp", 0, 0)

    grads = local(
        turn_kernel,
        [((YLO, block, tokens), narrow)] * ZH,
        1,
        scratch_shapes=[pltpu.VMEM((YLO * ZH * block, tokens), narrow)],
    )(zh[None], out_grad.reshape(tokens, YLO * ZH * block))
    near = [shift(grads[step], "zh", ZH, step) for step in (1, 3)]
    far = shift(grads[2], "zh", ZH, 2)

    piece = pieces.astype(wide).sum(0).astype(narrow)
    piece = jnp.stack([piece] + [shift(piece, "zh", ZH, step) for step in range(1, ZH)])
    piece, near = lax.optimization_barrier((piece, near))
    projected = lax.all_to_all(jnp.broadcast_to(piece, (n_fsdp,) + piece.shape), "fsdp", 0, 0)

    grads = [g.reshape(YLO, ZL, CORE, cols, tokens) for g in (grads[0], near[0], far, near[1])]
    place = jnp.stack([ylo, zl, core])
    one = (cols, rank)
    (sent,) = gradient_call(send_kernel, [((YLO * ZL,) + one, narrow)], tokens, cols, 0)(
        place, projected, *grads
    )
    came = swap(sent, "core")
    own, over_y, over_z, over_both = gradient_call(
        keep_kernel, [(one, wide)] + [(one, narrow)] * 3, tokens, cols, 1
    )(place, projected, *grads, came)
    over_both = lax.ppermute(over_both, ("ylo", "zl"), [(i, 3 - i) for i in range(4)])
    over_y, over_z = swap(over_y, "ylo"), swap(over_z, "zl")
    gradient = own + over_y.astype(wide) + over_z.astype(wide) + over_both.astype(wide)
    gradient = gradient[None]

    first_new = 0.9 * first_moment + 0.1 * gradient
    second_new = 0.999 * second_moment + 0.001 * gradient * gradient
    direction = (first_new / bias_first / (jnp.sqrt(second_new / bias_second) + epsilon)).astype(narrow)
    direction = lax.all_to_all(jnp.broadcast_to(direction, (n_fsdp, cols, rank)), "fsdp", 0, 0)
    weight_update = lax.dot_general(
        direction, projector, (((2,), (1,)), ((), ())), preferred_element_type=wide
    ).astype(narrow)
    return (weight_update, first_new, second_new)


def solution(mesh):
    fine = Mesh(
        mesh.devices.reshape(YLO, ZH, ZL, CORE, mesh.devices.shape[1]), DP + ("fsdp",)
    )
    in_specs = (
        P(DP, "fsdp"),
        P("fsdp", None),
        P(DP, "fsdp", None),
        P("fsdp", DP, None),
        P("fsdp", DP, None),
    )
    out_specs = (P(None, DP, "fsdp"), P("fsdp", DP, None), P("fsdp", DP, None))
    return jax.shard_map(shards, mesh=fine, in_specs=in_specs, out_specs=out_specs, check_vma=False)
```

```python
import functools

import jax
import jax.numpy as jnp
from jax import lax
from jax.experimental import pallas as pl
from jax.experimental.pallas import tpu as pltpu
from jax.sharding import Mesh, PartitionSpec as P

bias_first = 1.0 - 0.9**20
bias_second = 1.0 - 0.999**20
epsilon = 1e-08

YLO, ZH, ZL, CORE = 2, 4, 2, 2
DP = ("ylo", "zh", "zl", "core")
YHI, X = 2, 4
FSDP = ("yhi", "x")
wide, narrow = jnp.float32, jnp.bfloat16
VMEM = pl.BlockSpec(memory_space=pltpu.VMEM)
SMEM = pl.BlockSpec(memory_space=pltpu.SMEM)


def swap(value, axis):
    return lax.ppermute(value, axis, [(0, 1), (1, 0)])


def shift(value, axis, size, step):
    return lax.ppermute(value, axis, [(i, (i + step) % size) for i in range(size)])


def local(body, outs, count, **kwargs):
    return pl.pallas_call(
        body,
        out_shape=[jax.ShapeDtypeStruct(shape, dtype) for shape, dtype in outs],
        in_specs=[SMEM] + [VMEM] * count,
        out_specs=[VMEM] * len(outs),
        compiler_params=pltpu.CompilerParams(vmem_limit_bytes=16 * 2**20),
        **kwargs,
    )


def turn_kernel(zh_ref, grads_ref, *refs):
    outs, turned = refs[:ZH], refs[ZH]
    turned[...] = grads_ref[...].T
    block = outs[0].shape[1]
    for step in range(ZH):
        owner = lax.rem(zh_ref[0] + step, ZH)
        for y in range(YLO):
            start = pl.multiple_of((y * ZH + owner) * block, 16)
            outs[step][y] = turned[pl.ds(start, block), :]


def product(place_ref, core, pieces, grads, whole):
    cols, tokens = grads[0].shape[3:]
    for j, piece in enumerate(pieces):
        whole[:, pl.ds(place_ref[3 + j], 1)] = piece[...][:, None]
    rows = []
    for part in range(YLO * ZL):
        y = lax.rem(place_ref[0] + part % 2, YLO)
        z = lax.rem(place_ref[1] + part // 2, ZL)
        rows.append(jnp.concatenate([grads[step][y, z, core] for step in range(ZH)], axis=1))
    total = jnp.dot(
        jnp.concatenate(rows, axis=0),
        whole[...].reshape(ZH * tokens, whole.shape[-1]),
        preferred_element_type=wide,
    )
    return total.reshape(YLO * ZL, cols, -1)


def send_kernel(place_ref, *refs):
    pieces, grads, (out_ref, whole) = refs[:8], refs[8 : 8 + ZH], refs[8 + ZH :]
    out_ref[...] = product(place_ref, 1 - place_ref[2], pieces, grads, whole).astype(narrow)


def keep_kernel(place_ref, *refs):
    pieces, grads, rest = refs[:8], refs[8 : 8 + ZH], refs[8 + ZH :]
    came_ref, own_ref, *sent_refs, whole = rest
    total = product(place_ref, place_ref[2], pieces, grads, whole) + came_ref[...].astype(wide)
    own_ref[...] = total[0]
    for part, ref in enumerate(sent_refs):
        ref[...] = total[part + 1].astype(narrow)


def gradient_call(body, outs, tokens, rank, extra):
    n_fsdp = YHI * X
    return pl.pallas_call(
        body,
        out_shape=[jax.ShapeDtypeStruct(shape, dtype) for shape, dtype in outs],
        in_specs=[SMEM] + [VMEM] * (n_fsdp + ZH + extra),
        out_specs=[VMEM] * len(outs),
        scratch_shapes=[pltpu.VMEM((ZH, n_fsdp, tokens // n_fsdp, rank), narrow)],
        compiler_params=pltpu.CompilerParams(vmem_limit_bytes=16 * 2**20),
    )


def adam_kernel(own_ref, over_y_ref, over_z_ref, over_both_ref, first_ref, second_ref, *outs):
    gradient = own_ref[...] + over_y_ref[...].astype(wide)
    gradient = gradient + over_z_ref[...].astype(wide) + over_both_ref[...].astype(wide)
    first_new = 0.9 * first_ref[0] + 0.1 * gradient
    second_new = 0.999 * second_ref[0] + 0.001 * gradient * gradient
    root = jnp.sqrt(second_new / bias_second) + epsilon
    outs[0][...] = (first_new / bias_first / root).astype(narrow)
    outs[1][0] = first_new
    outs[2][0] = second_new


def back_kernel(count, first, place_ref, projector_ref, *refs):
    blocks = refs[:count]
    out_ref, held, sems = refs[-3:]
    stacked = jnp.concatenate([block[...] for block in blocks], axis=0)
    held[...] = lax.dot_general(
        stacked, projector_ref[...], (((1,), (1,)), ((), ())), preferred_element_type=wide
    ).astype(narrow).reshape(held.shape)
    copies = [
        pltpu.make_async_copy(held.at[j], out_ref.at[place_ref[3 + first + j]], sems.at[j])
        for j in range(count)
    ]
    for copy in copies:
        copy.start()
    for copy in copies:
        copy.wait()


def back(place, projector, blocks, first, out):
    count = len(blocks)
    cols = blocks[0].shape[0]
    width = projector.shape[0]
    before = [] if out is None else [out]
    return pl.pallas_call(
        functools.partial(back_kernel, count, first),
        out_shape=jax.ShapeDtypeStruct((YHI * X, cols, width), narrow),
        in_specs=[SMEM] + [VMEM] * (1 + count) + [pl.BlockSpec(memory_space=pl.ANY)] * len(before),
        out_specs=pl.BlockSpec(memory_space=pl.ANY),
        input_output_aliases={} if out is None else {2 + count: 0},
        scratch_shapes=[
            pltpu.VMEM((count, cols, width), narrow),
            pltpu.SemaphoreType.DMA((count,)),
        ],
        compiler_params=pltpu.CompilerParams(vmem_limit_bytes=16 * 2**20),
    )(place, projector, *blocks, *before)


def gathered(value, other=None):
    other = swap(value, "yhi") if other is None else other
    steps = (1, 3, 2)
    return (
        [value, other]
        + [shift(value, "x", X, step) for step in steps]
        + [shift(other, "x", X, step) for step in steps]
    )


def gathered_from(yhi, x):
    mine, other = yhi * X, (1 - yhi) * X
    steps = [(x + X - step) % X for step in (1, 3, 2)]
    return [mine + x, other + x] + [mine + s for s in steps] + [other + s for s in steps]


def shards(activations, projector, out_grad, first_moment, second_moment):
    n_fsdp = YHI * X
    zh, zl, core, ylo, yhi, x = (
        lax.axis_index(a) for a in ("zh", "zl", "core", "ylo", "yhi", "x")
    )
    tokens, rank = activations.shape[0], projector.shape[1]
    cols = first_moment.shape[1]
    block = ZL * CORE * cols

    partial_value = jnp.dot(activations, projector, preferred_element_type=wide).astype(narrow)
    partial_value, out_grad = lax.optimization_barrier((partial_value, out_grad))
    pieces = lax.all_to_all(partial_value.reshape(n_fsdp, tokens // n_fsdp, rank), FSDP, 0, 0)

    grads = local(
        turn_kernel,
        [((YLO, block, tokens), narrow)] * ZH,
        1,
        scratch_shapes=[pltpu.VMEM((YLO * ZH * block, tokens), narrow)],
    )(zh[None], out_grad.reshape(tokens, YLO * ZH * block))
    near = [shift(grads[step], "zh", ZH, step) for step in (1, 3)]

    piece = pieces.astype(wide).sum(0).astype(narrow)
    piece = jnp.stack([piece] + [shift(piece, "zh", ZH, step) for step in range(1, ZH)])
    piece, near = lax.optimization_barrier((piece, near))
    other, late = lax.optimization_barrier((swap(piece, "yhi"), grads[2]))
    far = shift(late, "zh", ZH, 2)
    projected = gathered(piece, other)

    grads = [g.reshape(YLO, ZL, CORE, cols, tokens) for g in (grads[0], near[0], far, near[1])]
    place = jnp.stack([ylo, zl, core] + gathered_from(yhi, x))
    one = (cols, rank)
    (sent,) = gradient_call(send_kernel, [((YLO * ZL,) + one, narrow)], tokens, rank, 0)(
        place, *projected, *grads
    )
    came = swap(sent, "core")
    own, over_y, over_z, over_both = gradient_call(
        keep_kernel, [(one, wide)] + [(one, narrow)] * 3, tokens, rank, 1
    )(place, *projected, *grads, came)
    over_both = lax.ppermute(over_both, ("ylo", "zl"), [(i, 3 - i) for i in range(4)])
    over_y, over_z = swap(over_y, "ylo"), swap(over_z, "zl")
    moment = jax.ShapeDtypeStruct((1,) + one, wide)
    direction, first_new, second_new = pl.pallas_call(
        adam_kernel,
        out_shape=[jax.ShapeDtypeStruct(one, narrow), moment, moment],
        in_specs=[VMEM] * 6,
        out_specs=[VMEM] * 3,
        compiler_params=pltpu.CompilerParams(vmem_limit_bytes=16 * 2**20),
    )(own, over_y, over_z, over_both, first_moment, second_moment)
    directions = gathered(direction)
    weight_update = back(place, projector, directions[:5], 0, None)
    weight_update = back(place, projector, directions[5:], 5, weight_update)
    return (weight_update, first_new, second_new)


def solution(mesh):
    fine = Mesh(
        mesh.devices.reshape(YLO, ZH, ZL, CORE, YHI, X), DP + FSDP
    )
    in_specs = (
        P(DP, FSDP),
        P(FSDP, None),
        P(DP, FSDP, None),
        P(FSDP, DP, None),
        P(FSDP, DP, None),
    )
    out_specs = (P(None, DP, FSDP), P(FSDP, DP, None), P(FSDP, DP, None))
    return jax.shard_map(shards, mesh=fine, in_specs=in_specs, out_specs=out_specs, check_vma=False)
```

```python
import functools

import jax
import jax.numpy as jnp
from jax import lax
from jax.experimental import pallas as pl
from jax.experimental.pallas import tpu as pltpu
from jax.sharding import Mesh, PartitionSpec as P

bias_first = 1.0 - 0.9**20
bias_second = 1.0 - 0.999**20
epsilon = 1e-08

YLO, ZH, ZL, CORE = 2, 4, 2, 2
DP = ("ylo", "zh", "zl", "core")
YHI, X = 2, 4
FSDP = ("yhi", "x")
wide, narrow = jnp.float32, jnp.bfloat16
VMEM = pl.BlockSpec(memory_space=pltpu.VMEM)
SMEM = pl.BlockSpec(memory_space=pltpu.SMEM)


def swap(value, axis):
    return lax.ppermute(value, axis, [(0, 1), (1, 0)])


def shift(value, axis, size, step):
    return lax.ppermute(value, axis, [(i, (i + step) % size) for i in range(size)])


def local(body, outs, count, **kwargs):
    return pl.pallas_call(
        body,
        out_shape=[jax.ShapeDtypeStruct(shape, dtype) for shape, dtype in outs],
        in_specs=[SMEM] + [VMEM] * count,
        out_specs=[VMEM] * len(outs),
        compiler_params=pltpu.CompilerParams(vmem_limit_bytes=16 * 2**20),
        **kwargs,
    )


def turn_kernel(zh_ref, grads_ref, *refs):
    outs, turned = refs[:ZH], refs[ZH]
    turned[...] = grads_ref[...].T
    block = outs[0].shape[1]
    for step in range(ZH):
        owner = lax.rem(zh_ref[0] + step, ZH)
        for y in range(YLO):
            start = pl.multiple_of((y * ZH + owner) * block, 16)
            outs[step][y] = turned[pl.ds(start, block), :]


def product(place_ref, core, pieces, grads, whole):
    cols, tokens = grads[0].shape[3:]
    for j, piece in enumerate(pieces):
        whole[:, pl.ds(place_ref[3 + j], 1)] = piece[...][:, None]
    rows = []
    for part in range(YLO * ZL):
        y = lax.rem(place_ref[0] + part % 2, YLO)
        z = lax.rem(place_ref[1] + part // 2, ZL)
        rows.append(jnp.concatenate([grads[step][y, z, core] for step in range(ZH)], axis=1))
    total = jnp.dot(
        jnp.concatenate(rows, axis=0),
        whole[...].reshape(ZH * tokens, whole.shape[-1]),
        preferred_element_type=wide,
    )
    return total.reshape(YLO * ZL, cols, -1)


def send_kernel(place_ref, *refs):
    pieces, grads, (out_ref, whole) = refs[:8], refs[8 : 8 + ZH], refs[8 + ZH :]
    out_ref[...] = product(place_ref, 1 - place_ref[2], pieces, grads, whole).astype(narrow)


def keep_kernel(place_ref, *refs):
    pieces, grads, rest = refs[:8], refs[8 : 8 + ZH], refs[8 + ZH :]
    came_ref, own_ref, *sent_refs, whole = rest
    total = product(place_ref, place_ref[2], pieces, grads, whole) + came_ref[...].astype(wide)
    own_ref[...] = total[0]
    for part, ref in enumerate(sent_refs):
        ref[...] = total[part + 1].astype(narrow)


def gradient_call(body, outs, tokens, rank, extra):
    n_fsdp = YHI * X
    return pl.pallas_call(
        body,
        out_shape=[jax.ShapeDtypeStruct(shape, dtype) for shape, dtype in outs],
        in_specs=[SMEM] + [VMEM] * (n_fsdp + ZH + extra),
        out_specs=[VMEM] * len(outs),
        scratch_shapes=[pltpu.VMEM((ZH, n_fsdp, tokens // n_fsdp, rank), narrow)],
        compiler_params=pltpu.CompilerParams(vmem_limit_bytes=16 * 2**20),
    )


def adam_kernel(own_ref, over_both_ref, over_z_ref, over_y_ref, first_ref, second_ref, *outs):
    gradient = own_ref[...] + over_y_ref[...].astype(wide)
    gradient = gradient + over_z_ref[...].astype(wide) + over_both_ref[...].astype(wide)
    first_new = 0.9 * first_ref[0] + 0.1 * gradient
    second_new = 0.999 * second_ref[0] + 0.001 * gradient * gradient
    root = jnp.sqrt(second_new / bias_second) + epsilon
    outs[0][...] = (first_new / bias_first / root).astype(narrow)
    outs[1][0] = first_new
    outs[2][0] = second_new


def back_kernel(count, first, place_ref, projector_ref, *refs):
    blocks = refs[:count]
    out_ref, held, sems = refs[-3:]
    stacked = jnp.concatenate([block[...] for block in blocks], axis=0)
    held[...] = lax.dot_general(
        stacked, projector_ref[...], (((1,), (1,)), ((), ())), preferred_element_type=wide
    ).astype(narrow).reshape(held.shape)
    copies = [
        pltpu.make_async_copy(held.at[j], out_ref.at[place_ref[3 + first + j]], sems.at[j])
        for j in range(count)
    ]
    for copy in copies:
        copy.start()
    for copy in copies:
        copy.wait()


def back(place, projector, blocks, first, out):
    count = len(blocks)
    cols = blocks[0].shape[0]
    width = projector.shape[0]
    before = [] if out is None else [out]
    return pl.pallas_call(
        functools.partial(back_kernel, count, first),
        out_shape=jax.ShapeDtypeStruct((YHI * X, cols, width), narrow),
        in_specs=[SMEM] + [VMEM] * (1 + count) + [pl.BlockSpec(memory_space=pl.ANY)] * len(before),
        out_specs=pl.BlockSpec(memory_space=pl.ANY),
        input_output_aliases={} if out is None else {2 + count: 0},
        scratch_shapes=[
            pltpu.VMEM((count, cols, width), narrow),
            pltpu.SemaphoreType.DMA((count,)),
        ],
        compiler_params=pltpu.CompilerParams(vmem_limit_bytes=16 * 2**20),
    )(place, projector, *blocks, *before)


def gathered(value, other=None):
    other = swap(value, "yhi") if other is None else other
    mine = [shift(value, "x", X, step) for step in (1, 3, 2)]
    rest = [shift(other, "x", X, step) for step in (1, 3)] + [swap(mine[2], "yhi")]
    return [value, other] + mine + rest


def gathered_from(yhi, x):
    mine, other = yhi * X, (1 - yhi) * X
    steps = [(x + X - step) % X for step in (1, 3, 2)]
    return [mine + x, other + x] + [mine + s for s in steps] + [other + s for s in steps]


def shards(activations, projector, out_grad, first_moment, second_moment):
    n_fsdp = YHI * X
    zh, zl, core, ylo, yhi, x = (
        lax.axis_index(a) for a in ("zh", "zl", "core", "ylo", "yhi", "x")
    )
    tokens, rank = activations.shape[0], projector.shape[1]
    cols = first_moment.shape[1]
    block = ZL * CORE * cols

    partial_value = jnp.dot(activations, projector, preferred_element_type=wide).astype(narrow)
    partial_value, out_grad = lax.optimization_barrier((partial_value, out_grad))
    pieces = lax.all_to_all(partial_value.reshape(n_fsdp, tokens // n_fsdp, rank), FSDP, 0, 0)

    grads = local(
        turn_kernel,
        [((YLO, block, tokens), narrow)] * ZH,
        1,
        scratch_shapes=[pltpu.VMEM((YLO * ZH * block, tokens), narrow)],
    )(zh[None], out_grad.reshape(tokens, YLO * ZH * block))
    near = [shift(grads[step], "zh", ZH, step) for step in (1, 3)]

    piece = pieces.astype(wide).sum(0).astype(narrow)
    piece = jnp.stack([piece] + [shift(piece, "zh", ZH, step) for step in range(1, ZH)])
    piece, near = lax.optimization_barrier((piece, near))
    other, late = lax.optimization_barrier((swap(piece, "yhi"), grads[2]))
    far = shift(late, "zh", ZH, 2)
    projected = gathered(piece, other)

    grads = [g.reshape(YLO, ZL, CORE, cols, tokens) for g in (grads[0], near[0], far, near[1])]
    place = jnp.stack([ylo, zl, core] + gathered_from(yhi, x))
    one = (cols, rank)
    (sent,) = gradient_call(send_kernel, [((YLO * ZL,) + one, narrow)], tokens, rank, 0)(
        place, *projected, *grads
    )
    came = swap(sent, "core")
    own, over_y, over_z, over_both = gradient_call(
        keep_kernel, [(one, wide)] + [(one, narrow)] * 3, tokens, rank, 1
    )(place, *projected, *grads, came)
    over_y, over_z = swap(over_y, "ylo"), swap(over_z, "zl")
    over_both = lax.ppermute(over_both, ("ylo", "zl"), [(i, 3 - i) for i in range(4)])
    moment = jax.ShapeDtypeStruct((1,) + one, wide)
    direction, first_new, second_new = pl.pallas_call(
        adam_kernel,
        out_shape=[jax.ShapeDtypeStruct(one, narrow), moment, moment],
        in_specs=[VMEM] * 6,
        out_specs=[VMEM] * 3,
        compiler_params=pltpu.CompilerParams(vmem_limit_bytes=16 * 2**20),
    )(own, over_both, over_z, over_y, first_moment, second_moment)
    directions = gathered(direction)
    weight_update = back(place, projector, directions[:5], 0, None)
    weight_update = back(place, projector, directions[5:], 5, weight_update)
    return (weight_update, first_new, second_new)


def solution(mesh):
    fine = Mesh(
        mesh.devices.reshape(YLO, ZH, ZL, CORE, YHI, X), DP + FSDP
    )
    in_specs = (
        P(DP, FSDP),
        P(FSDP, None),
        P(DP, FSDP, None),
        P(FSDP, DP, None),
        P(FSDP, DP, None),
    )
    out_specs = (P(None, DP, FSDP), P(FSDP, DP, None), P(FSDP, DP, None))
    return jax.shard_map(shards, mesh=fine, in_specs=in_specs, out_specs=out_specs, check_vma=False)
```

```python
import functools

import jax
import jax.numpy as jnp
from jax import lax
from jax.experimental import pallas as pl
from jax.experimental.pallas import tpu as pltpu
from jax.sharding import Mesh, PartitionSpec as P

bias_first = 1.0 - 0.9**20
bias_second = 1.0 - 0.999**20
epsilon = 1e-08

YLO, ZH, ZL, CORE = 2, 4, 2, 2
PARTS = YLO * ZL
DP = ("ylo", "zh", "zl", "core")
YHI, X = 2, 4
FSDP = ("yhi", "x")
wide, narrow = jnp.float32, jnp.bfloat16
VMEM = pl.BlockSpec(memory_space=pltpu.VMEM)
SMEM = pl.BlockSpec(memory_space=pltpu.SMEM)


def swap(value, axis):
    return lax.ppermute(value, axis, [(0, 1), (1, 0)])


def shift(value, axis, size, step):
    return lax.ppermute(value, axis, [(i, (i + step) % size) for i in range(size)])


def exchanged(over_y, over_z, over_both):
    both = lax.ppermute(over_both, ("ylo", "zl"), [(i, 3 - i) for i in range(4)])
    return [swap(over_y, "ylo"), swap(over_z, "zl"), both]


def local(body, outs, count, **kwargs):
    return pl.pallas_call(
        body,
        out_shape=[jax.ShapeDtypeStruct(shape, dtype) for shape, dtype in outs],
        in_specs=[SMEM] + [VMEM] * count,
        out_specs=[VMEM] * len(outs),
        compiler_params=pltpu.CompilerParams(vmem_limit_bytes=16 * 2**20),
        **kwargs,
    )


def turn_kernel(place_ref, grads_ref, *refs):
    outs, turned = refs[:PARTS], refs[PARTS]
    turned[...] = grads_ref[...].T
    block = outs[0].shape[1]
    for part in range(PARTS):
        y = lax.rem(place_ref[0] + part % 2, YLO)
        z = lax.rem(place_ref[1] + part // 2, ZL)
        for h in range(ZH):
            start = pl.multiple_of(((y * ZH + h) * ZL + z) * block, 16)
            outs[part][h] = turned[pl.ds(start, block), :]


def product(place_ref, core, pieces, grads, whole):
    cols, tokens = grads[0].shape[2:]
    for j, piece in enumerate(pieces):
        whole[:, pl.ds(place_ref[4 + YHI * X + j], 1)] = piece[...][:, None]
    rows = []
    for step in range(ZH):
        h = lax.rem(place_ref[2] + step, ZH)
        rows.append(jnp.concatenate([part[h, core] for part in grads], axis=1))
    total = jnp.dot(
        jnp.concatenate(rows, axis=0),
        whole[...].reshape(PARTS * tokens, whole.shape[-1]),
        preferred_element_type=wide,
    )
    return total.reshape(ZH, cols, -1)


def send_kernel(place_ref, *refs):
    pieces, grads, (out_ref, whole) = refs[:X], refs[X : X + PARTS], refs[X + PARTS :]
    out_ref[...] = product(place_ref, 1 - place_ref[3], pieces, grads, whole).astype(narrow)


def keep_kernel(place_ref, *refs):
    pieces, grads, rest = refs[:X], refs[X : X + PARTS], refs[X + PARTS :]
    came_ref, own_ref, up_far_ref, down_far_ref, up_ref, down_ref, up_held_ref, down_held_ref, whole = rest
    total = product(place_ref, place_ref[3], pieces, grads, whole) + came_ref[...].astype(wide)
    lanes = total.shape[-1] // 2
    own_ref[...] = total[0]
    up_far_ref[...] = total[2, :, :lanes].astype(narrow)
    down_far_ref[...] = total[2, :, lanes:].astype(narrow)
    up_ref[...] = total[1, :, lanes:].astype(narrow)
    down_ref[...] = total[3, :, :lanes].astype(narrow)
    up_held_ref[...] = total[1, :, :lanes]
    down_held_ref[...] = total[3, :, lanes:]


def relay_kernel(up_held_ref, down_held_ref, up_ref, down_ref, up_out_ref, down_out_ref):
    up_out_ref[...] = (up_held_ref[...] + up_ref[...].astype(wide)).astype(narrow)
    down_out_ref[...] = (down_held_ref[...] + down_ref[...].astype(wide)).astype(narrow)


def gradient_call(body, outs, tokens, rank, extra):
    return pl.pallas_call(
        body,
        out_shape=[jax.ShapeDtypeStruct(shape, dtype) for shape, dtype in outs],
        in_specs=[SMEM] + [VMEM] * (X + PARTS + extra),
        out_specs=[VMEM] * len(outs),
        scratch_shapes=[pltpu.VMEM((PARTS, X, tokens // X, rank), narrow)],
        compiler_params=pltpu.CompilerParams(vmem_limit_bytes=16 * 2**20),
    )


def adam_kernel(own_ref, up_ref, down_ref, up_sum_ref, down_sum_ref, first_ref, second_ref, *outs):
    left = down_ref[...].astype(wide) + up_sum_ref[...].astype(wide)
    right = up_ref[...].astype(wide) + down_sum_ref[...].astype(wide)
    gradient = own_ref[...] + jnp.concatenate([left, right], axis=1)
    first_new = 0.9 * first_ref[0] + 0.1 * gradient
    second_new = 0.999 * second_ref[0] + 0.001 * gradient * gradient
    root = jnp.sqrt(second_new / bias_second) + epsilon
    outs[0][...] = (first_new / bias_first / root).astype(narrow)
    outs[1][0] = first_new
    outs[2][0] = second_new


def back_kernel(count, first, place_ref, projector_ref, *refs):
    blocks = refs[:count]
    out_ref, held, sems = refs[-3:]
    stacked = jnp.concatenate([block[...] for block in blocks], axis=0)
    held[...] = lax.dot_general(
        stacked, projector_ref[...], (((1,), (1,)), ((), ())), preferred_element_type=wide
    ).astype(narrow).reshape(held.shape)
    copies = [
        pltpu.make_async_copy(held.at[j], out_ref.at[place_ref[4 + first + j]], sems.at[j])
        for j in range(count)
    ]
    for copy in copies:
        copy.start()
    for copy in copies:
        copy.wait()


def back(place, projector, blocks, first, out):
    count = len(blocks)
    cols = blocks[0].shape[0]
    width = projector.shape[0]
    before = [] if out is None else [out]
    return pl.pallas_call(
        functools.partial(back_kernel, count, first),
        out_shape=jax.ShapeDtypeStruct((YHI * X, cols, width), narrow),
        in_specs=[SMEM] + [VMEM] * (1 + count) + [pl.BlockSpec(memory_space=pl.ANY)] * len(before),
        out_specs=pl.BlockSpec(memory_space=pl.ANY),
        input_output_aliases={} if out is None else {2 + count: 0},
        scratch_shapes=[
            pltpu.VMEM((count, cols, width), narrow),
            pltpu.SemaphoreType.DMA((count,)),
        ],
        compiler_params=pltpu.CompilerParams(vmem_limit_bytes=16 * 2**20),
    )(place, projector, *blocks, *before)


def gathered(value, other=None):
    other = swap(value, "yhi") if other is None else other
    mine = [shift(value, "x", X, step) for step in (1, 3, 2)]
    rest = [shift(other, "x", X, step) for step in (1, 3)] + [swap(mine[2], "yhi")]
    return [value, other] + mine + rest


def gathered_from(yhi, x):
    mine, other = yhi * X, (1 - yhi) * X
    steps = [(x + X - step) % X for step in (1, 3, 2)]
    return [mine + x, other + x] + [mine + s for s in steps] + [other + s for s in steps]


def shards(activations, projector, out_grad, first_moment, second_moment):
    n_fsdp = YHI * X
    zh, zl, core, ylo, yhi, x = (
        lax.axis_index(a) for a in ("zh", "zl", "core", "ylo", "yhi", "x")
    )
    tokens, rank = activations.shape[0], projector.shape[1]
    cols = first_moment.shape[1]
    block = CORE * cols
    sources = [(x + X - step) % X for step in (0, 1, 3, 2)]
    place = jnp.stack([ylo, zl, zh, core] + gathered_from(yhi, x) + sources)

    partial_value = jnp.dot(activations, projector, preferred_element_type=wide).astype(narrow)
    partial_value, out_grad = lax.optimization_barrier((partial_value, out_grad))
    share = partial_value.reshape(1, X, tokens // X, rank)
    pieces = lax.all_to_all(
        jnp.broadcast_to(share, (YHI,) + share.shape[1:]).reshape((n_fsdp,) + share.shape[2:]),
        FSDP,
        0,
        0,
    )

    grads = local(
        turn_kernel,
        [((ZH, block, tokens), narrow)] * PARTS,
        1,
        scratch_shapes=[pltpu.VMEM((YLO * ZH * ZL * block, tokens), narrow)],
    )(place, out_grad.reshape(tokens, YLO * ZH * ZL * block))
    moved = exchanged(*grads[1:])
    piece = pieces.astype(wide).sum(0).astype(narrow)
    piece = jnp.stack([piece] + exchanged(piece, piece, piece))
    piece, moved[:2] = lax.optimization_barrier((piece, moved[:2]))
    projected = [piece] + [shift(piece, "x", X, step) for step in (1, 3, 2)]
    grads = [g.reshape(ZH, CORE, cols, tokens) for g in [grads[0]] + moved]
    one = (cols, rank)
    (sent,) = gradient_call(send_kernel, [((ZH,) + one, narrow)], tokens, rank, 0)(
        place, *projected, *grads
    )
    came = swap(sent, "core")
    part = (cols, rank // 2)
    own, up_far, down_far, up, down, up_held, down_held = gradient_call(
        keep_kernel,
        [(one, wide)] + [(part, narrow)] * 4 + [(part, wide)] * 2,
        tokens,
        rank,
        1,
    )(place, *projected, *grads, came)
    up_far, down_far = shift(up_far, "zh", ZH, 1), shift(down_far, "zh", ZH, 3)
    up, down = shift(up, "zh", ZH, 1), shift(down, "zh", ZH, 3)
    up_sum, down_sum = pl.pallas_call(
        relay_kernel,
        out_shape=[jax.ShapeDtypeStruct(part, narrow)] * 2,
        in_specs=[VMEM] * 4,
        out_specs=[VMEM] * 2,
        compiler_params=pltpu.CompilerParams(vmem_limit_bytes=16 * 2**20),
    )(up_held, down_held, up_far, down_far)
    up_sum, down_sum = shift(up_sum, "zh", ZH, 1), shift(down_sum, "zh", ZH, 3)
    moment = jax.ShapeDtypeStruct((1,) + one, wide)
    direction, first_new, second_new = pl.pallas_call(
        adam_kernel,
        out_shape=[jax.ShapeDtypeStruct(one, narrow), moment, moment],
        in_specs=[VMEM] * 7,
        out_specs=[VMEM] * 3,
        compiler_params=pltpu.CompilerParams(vmem_limit_bytes=16 * 2**20),
    )(own, up, down, up_sum, down_sum, first_moment, second_moment)
    directions = gathered(direction)
    weight_update = back(place, projector, directions[:5], 0, None)
    weight_update = back(place, projector, directions[5:], 5, weight_update)
    return (weight_update, first_new, second_new)


def solution(mesh):
    fine = Mesh(
        mesh.devices.reshape(YLO, ZH, ZL, CORE, YHI, X), DP + FSDP
    )
    in_specs = (
        P(DP, FSDP),
        P(FSDP, None),
        P(DP, FSDP, None),
        P(FSDP, DP, None),
        P(FSDP, DP, None),
    )
    out_specs = (P(None, DP, FSDP), P(FSDP, DP, None), P(FSDP, DP, None))
    return jax.shard_map(shards, mesh=fine, in_specs=in_specs, out_specs=out_specs, check_vma=False)
```

```python
import functools

import jax
import jax.numpy as jnp
from jax import lax
from jax.experimental import pallas as pl
from jax.experimental.pallas import tpu as pltpu
from jax.sharding import Mesh, PartitionSpec as P

bias_first = 1.0 - 0.9**20
bias_second = 1.0 - 0.999**20
epsilon = 1e-08

YLO, ZH, ZL, CORE = 2, 4, 2, 2
PARTS = YLO * ZL
DP = ("ylo", "zh", "zl", "core")
YHI, X = 2, 4
FSDP = ("yhi", "x")
wide, narrow = jnp.float32, jnp.bfloat16
VMEM = pl.BlockSpec(memory_space=pltpu.VMEM)
SMEM = pl.BlockSpec(memory_space=pltpu.SMEM)


def swap(value, axis):
    return lax.ppermute(value, axis, [(0, 1), (1, 0)])


def shift(value, axis, size, step):
    return lax.ppermute(value, axis, [(i, (i + step) % size) for i in range(size)])


def exchanged(over_y, over_z, over_both):
    both = lax.ppermute(over_both, ("ylo", "zl"), [(i, 3 - i) for i in range(4)])
    return [swap(over_y, "ylo"), swap(over_z, "zl"), both]


def local(body, outs, count, **kwargs):
    return pl.pallas_call(
        body,
        out_shape=[jax.ShapeDtypeStruct(shape, dtype) for shape, dtype in outs],
        in_specs=[SMEM] + [VMEM] * count,
        out_specs=[VMEM] * len(outs),
        compiler_params=pltpu.CompilerParams(vmem_limit_bytes=16 * 2**20),
        **kwargs,
    )


def turn_kernel(place_ref, grads_ref, *refs):
    outs, turned = refs[:PARTS], refs[PARTS]
    turned[...] = grads_ref[...].T
    block = outs[0].shape[1]
    for part in range(PARTS):
        y = lax.rem(place_ref[0] + part % 2, YLO)
        z = lax.rem(place_ref[1] + part // 2, ZL)
        for h in range(ZH):
            start = pl.multiple_of(((y * ZH + h) * ZL + z) * block, 16)
            outs[part][h] = turned[pl.ds(start, block), :]


def product(place_ref, core, grads, whole):
    cols, tokens = grads[0].shape[2:]
    rows = []
    for step in range(ZH):
        h = lax.rem(place_ref[2] + step, ZH)
        rows.append(jnp.concatenate([part[h, core] for part in grads], axis=1))
    total = jnp.dot(
        jnp.concatenate(rows, axis=0),
        whole[...].reshape(PARTS * tokens, whole.shape[-1]),
        preferred_element_type=wide,
    )
    return total.reshape(ZH, cols, -1)


def send_kernel(place_ref, *refs):
    pieces, grads, (out_ref, whole) = refs[:X], refs[X : X + PARTS], refs[X + PARTS :]
    for j, piece in enumerate(pieces):
        whole[:, pl.ds(place_ref[4 + YHI * X + j], 1)] = piece[...][:, None]
    out_ref[...] = product(place_ref, 1 - place_ref[3], grads, whole).astype(narrow)


def keep_kernel(place_ref, whole, *refs):
    grads, out_ref = refs[:PARTS], refs[PARTS]
    out_ref[...] = product(place_ref, place_ref[3], grads, whole)


def split_kernel(_, mine_ref, came_ref, *outs):
    own_ref, up_far_ref, down_far_ref, up_ref, down_ref, up_held_ref, down_held_ref = outs
    lanes = own_ref.shape[-1] // 2
    left, right = slice(0, lanes), slice(lanes, 2 * lanes)

    def total(step, half):
        return mine_ref[step, :, half] + came_ref[step, :, half].astype(wide)

    own_ref[:, left] = total(0, left)
    own_ref[:, right] = total(0, right)
    up_far_ref[...] = total(2, left).astype(narrow)
    down_far_ref[...] = total(2, right).astype(narrow)
    up_ref[...] = total(1, right).astype(narrow)
    down_ref[...] = total(3, left).astype(narrow)
    up_held_ref[...] = total(1, left)
    down_held_ref[...] = total(3, right)


def relay_kernel(up_held_ref, down_held_ref, up_ref, down_ref, up_out_ref, down_out_ref):
    up_out_ref[...] = (up_held_ref[...] + up_ref[...].astype(wide)).astype(narrow)
    down_out_ref[...] = (down_held_ref[...] + down_ref[...].astype(wide)).astype(narrow)


def adam_kernel(own_ref, up_ref, down_ref, up_sum_ref, down_sum_ref, first_ref, second_ref, *outs):
    left = down_ref[...].astype(wide) + up_sum_ref[...].astype(wide)
    right = up_ref[...].astype(wide) + down_sum_ref[...].astype(wide)
    gradient = own_ref[...] + jnp.concatenate([left, right], axis=1)
    first_new = 0.9 * first_ref[0] + 0.1 * gradient
    second_new = 0.999 * second_ref[0] + 0.001 * gradient * gradient
    root = jnp.sqrt(second_new / bias_second) + epsilon
    outs[0][...] = (first_new / bias_first / root).astype(narrow)
    outs[1][0] = first_new
    outs[2][0] = second_new


def back_kernel(count, first, place_ref, projector_ref, *refs):
    blocks = refs[:count]
    out_ref, held, sems = refs[-3:]
    stacked = jnp.concatenate([block[...] for block in blocks], axis=0)
    held[...] = lax.dot_general(
        stacked, projector_ref[...], (((1,), (1,)), ((), ())), preferred_element_type=wide
    ).astype(narrow).reshape(held.shape)
    copies = [
        pltpu.make_async_copy(held.at[j], out_ref.at[place_ref[4 + first + j]], sems.at[j])
        for j in range(count)
    ]
    for copy in copies:
        copy.start()
    for copy in copies:
        copy.wait()


def back(place, projector, blocks, first, out):
    count = len(blocks)
    cols = blocks[0].shape[0]
    width = projector.shape[0]
    before = [] if out is None else [out]
    return pl.pallas_call(
        functools.partial(back_kernel, count, first),
        out_shape=jax.ShapeDtypeStruct((YHI * X, cols, width), narrow),
        in_specs=[SMEM] + [VMEM] * (1 + count) + [pl.BlockSpec(memory_space=pl.ANY)] * len(before),
        out_specs=pl.BlockSpec(memory_space=pl.ANY),
        input_output_aliases={} if out is None else {2 + count: 0},
        scratch_shapes=[
            pltpu.VMEM((count, cols, width), narrow),
            pltpu.SemaphoreType.DMA((count,)),
        ],
        compiler_params=pltpu.CompilerParams(vmem_limit_bytes=16 * 2**20),
    )(place, projector, *blocks, *before)


def gathered(value, other=None):
    other = swap(value, "yhi") if other is None else other
    mine = [shift(value, "x", X, step) for step in (1, 3, 2)]
    rest = [shift(other, "x", X, step) for step in (1, 3)] + [swap(mine[2], "yhi")]
    return [value, other] + mine + rest


def gathered_from(yhi, x):
    mine, other = yhi * X, (1 - yhi) * X
    steps = [(x + X - step) % X for step in (1, 3, 2)]
    return [mine + x, other + x] + [mine + s for s in steps] + [other + s for s in steps]


def shards(activations, projector, out_grad, first_moment, second_moment):
    n_fsdp = YHI * X
    zh, zl, core, ylo, yhi, x = (
        lax.axis_index(a) for a in ("zh", "zl", "core", "ylo", "yhi", "x")
    )
    tokens, rank = activations.shape[0], projector.shape[1]
    cols = first_moment.shape[1]
    block = CORE * cols
    sources = [(x + X - step) % X for step in (0, 1, 3, 2)]
    place = jnp.stack([ylo, zl, zh, core] + gathered_from(yhi, x) + sources)

    partial_value = jnp.dot(activations, projector, preferred_element_type=wide).astype(narrow)
    partial_value, out_grad = lax.optimization_barrier((partial_value, out_grad))
    share = partial_value.reshape(1, X, tokens // X, rank)
    pieces = lax.all_to_all(
        jnp.broadcast_to(share, (YHI,) + share.shape[1:]).reshape((n_fsdp,) + share.shape[2:]),
        FSDP,
        0,
        0,
    )

    grads = local(
        turn_kernel,
        [((ZH, block, tokens), narrow)] * PARTS,
        1,
        scratch_shapes=[pltpu.VMEM((YLO * ZH * ZL * block, tokens), narrow)],
    )(place, out_grad.reshape(tokens, YLO * ZH * ZL * block))
    moved = exchanged(*grads[1:])
    piece = pieces.astype(wide).sum(0).astype(narrow)
    piece = jnp.stack([piece] + exchanged(piece, piece, piece))
    piece, moved[:2] = lax.optimization_barrier((piece, moved[:2]))
    projected = [piece] + [shift(piece, "x", X, step) for step in (1, 3, 2)]
    grads = [g.reshape(ZH, CORE, cols, tokens) for g in [grads[0]] + moved]
    one = (cols, rank)
    part = (cols, rank // 2)
    sent, whole = local(
        send_kernel,
        [((ZH,) + one, narrow), ((PARTS, X, tokens // X, rank), narrow)],
        X + PARTS,
    )(place, *projected, *grads)
    came = swap(sent, "core")
    (mine,) = local(keep_kernel, [((ZH,) + one, wide)], 1 + PARTS)(place, whole, *grads)
    own, up_far, down_far, up, down, up_held, down_held = local(
        split_kernel, [(one, wide)] + [(part, narrow)] * 4 + [(part, wide)] * 2, 2
    )(place, mine, came)
    up_far, down_far = shift(up_far, "zh", ZH, 1), shift(down_far, "zh", ZH, 3)
    up, down = shift(up, "zh", ZH, 1), shift(down, "zh", ZH, 3)
    up_sum, down_sum = pl.pallas_call(
        relay_kernel,
        out_shape=[jax.ShapeDtypeStruct(part, narrow)] * 2,
        in_specs=[VMEM] * 4,
        out_specs=[VMEM] * 2,
        compiler_params=pltpu.CompilerParams(vmem_limit_bytes=16 * 2**20),
    )(up_held, down_held, up_far, down_far)
    up_sum, down_sum = shift(up_sum, "zh", ZH, 1), shift(down_sum, "zh", ZH, 3)
    moment = jax.ShapeDtypeStruct((1,) + one, wide)
    direction, first_new, second_new = pl.pallas_call(
        adam_kernel,
        out_shape=[jax.ShapeDtypeStruct(one, narrow), moment, moment],
        in_specs=[VMEM] * 7,
        out_specs=[VMEM] * 3,
        compiler_params=pltpu.CompilerParams(vmem_limit_bytes=16 * 2**20),
    )(own, up, down, up_sum, down_sum, first_moment, second_moment)
    directions = gathered(direction)
    weight_update = back(place, projector, directions[:5], 0, None)
    weight_update = back(place, projector, directions[5:], 5, weight_update)
    return (weight_update, first_new, second_new)


def solution(mesh):
    fine = Mesh(
        mesh.devices.reshape(YLO, ZH, ZL, CORE, YHI, X), DP + FSDP
    )
    in_specs = (
        P(DP, FSDP),
        P(FSDP, None),
        P(DP, FSDP, None),
        P(FSDP, DP, None),
        P(FSDP, DP, None),
    )
    out_specs = (P(None, DP, FSDP), P(FSDP, DP, None), P(FSDP, DP, None))
    return jax.shard_map(shards, mesh=fine, in_specs=in_specs, out_specs=out_specs, check_vma=False)
```

```python
import functools

import jax
import jax.numpy as jnp
from jax import lax
from jax.experimental import pallas as pl
from jax.experimental.pallas import tpu as pltpu
from jax.sharding import Mesh, PartitionSpec as P

bias_first = 1.0 - 0.9**20
bias_second = 1.0 - 0.999**20
epsilon = 1e-08

YLO, ZH, ZL, CORE = 2, 4, 2, 2
PARTS = YLO * ZL
DP = ("ylo", "zh", "zl", "core")
YHI, X = 2, 4
CHUNKS = 2
FSDP = ("yhi", "x")
wide, narrow = jnp.float32, jnp.bfloat16
VMEM = pl.BlockSpec(memory_space=pltpu.VMEM)
SMEM = pl.BlockSpec(memory_space=pltpu.SMEM)


def swap(value, axis):
    return lax.ppermute(value, axis, [(0, 1), (1, 0)])


def shift(value, axis, size, step):
    return lax.ppermute(value, axis, [(i, (i + step) % size) for i in range(size)])


def exchanged(over_y, over_z, over_both):
    both = lax.ppermute(over_both, ("ylo", "zl"), [(i, 3 - i) for i in range(4)])
    return [swap(over_y, "ylo"), swap(over_z, "zl"), both]


def local(body, outs, count, **kwargs):
    return pl.pallas_call(
        body,
        out_shape=[jax.ShapeDtypeStruct(shape, dtype) for shape, dtype in outs],
        in_specs=[SMEM] + [VMEM] * count,
        out_specs=[VMEM] * len(outs),
        compiler_params=pltpu.CompilerParams(vmem_limit_bytes=16 * 2**20),
        **kwargs,
    )


def turn_kernel(place_ref, grads_ref, *refs):
    outs, turned = refs[:PARTS], refs[PARTS]
    turned[...] = grads_ref[...].T
    block = outs[0].shape[1]
    for part in range(PARTS):
        y = lax.rem(place_ref[0] + part % 2, YLO)
        z = lax.rem(place_ref[1] + part // 2, ZL)
        for h in range(ZH):
            start = pl.multiple_of(((y * ZH + h) * ZL + z) * block, 16)
            outs[part][h] = turned[pl.ds(start, block), :]


def product(place_ref, core, grads, whole):
    cols, tokens = grads[0].shape[2:]
    rows = []
    for step in range(ZH):
        h = lax.rem(place_ref[2] + step, ZH)
        rows.append(jnp.concatenate([part[h, core] for part in grads], axis=1))
    total = jnp.dot(
        jnp.concatenate(rows, axis=0),
        whole[...].reshape(PARTS * tokens, whole.shape[-1]),
        preferred_element_type=wide,
    )
    return total.reshape(ZH, cols, -1)


def send_kernel(place_ref, *refs):
    pieces, grads, (out_ref, whole) = refs[:X], refs[X : X + PARTS], refs[X + PARTS :]
    for j, piece in enumerate(pieces):
        whole[:, pl.ds(place_ref[4 + YHI * X + j], 1)] = piece[...][:, None]
    out_ref[...] = product(place_ref, 1 - place_ref[3], grads, whole).astype(narrow)


def keep_kernel(place_ref, whole, *refs):
    grads, out_ref = refs[:PARTS], refs[PARTS]
    out_ref[...] = product(place_ref, place_ref[3], grads, whole)


def split_kernel(_, mine_ref, came_ref, *outs):
    own_ref, up_far_ref, down_far_ref, up_ref, down_ref, up_held_ref, down_held_ref = outs
    lanes = own_ref.shape[-1] // 2
    left, right = slice(0, lanes), slice(lanes, 2 * lanes)

    def total(step, half):
        return mine_ref[step, :, half] + came_ref[step, :, half].astype(wide)

    own_ref[:, left] = total(0, left)
    own_ref[:, right] = total(0, right)
    up_far_ref[...] = total(2, left).astype(narrow)
    down_far_ref[...] = total(2, right).astype(narrow)
    up_ref[...] = total(1, right).astype(narrow)
    down_ref[...] = total(3, left).astype(narrow)
    up_held_ref[...] = total(1, left)
    down_held_ref[...] = total(3, right)


def relay_kernel(up_held_ref, down_held_ref, up_ref, down_ref, up_out_ref, down_out_ref):
    up_out_ref[...] = (up_held_ref[...] + up_ref[...].astype(wide)).astype(narrow)
    down_out_ref[...] = (down_held_ref[...] + down_ref[...].astype(wide)).astype(narrow)


def moments(own_ref, up_ref, down_ref, up_sum_ref, down_sum_ref, first_ref, second_ref):
    left = down_ref[...].astype(wide) + up_sum_ref[...].astype(wide)
    right = up_ref[...].astype(wide) + down_sum_ref[...].astype(wide)
    gradient = own_ref[...] + jnp.concatenate([left, right], axis=1)
    first_new = 0.9 * first_ref[0] + 0.1 * gradient
    second_new = 0.999 * second_ref[0] + 0.001 * gradient * gradient
    return first_new, second_new


def direction_kernel(*refs):
    first_new, second_new = moments(*refs[:7])
    root = jnp.sqrt(second_new / bias_second) + epsilon
    refs[7][...] = (first_new / bias_first / root).astype(narrow)


def moments_kernel(*refs):
    refs[7][0], refs[8][0] = moments(*refs[:7])


def back_kernel(count, first, place_ref, projector_ref, *refs):
    blocks = refs[:count]
    out_ref, held, sems = refs[-3:]
    stacked = jnp.concatenate([block[...] for block in blocks], axis=0)
    chunk = projector_ref.shape[0] // CHUNKS
    copies = []
    for c in range(CHUNKS):
        lanes = pl.ds(c * chunk, chunk)
        value = lax.dot_general(
            stacked, projector_ref[lanes, :], (((1,), (1,)), ((), ())), preferred_element_type=wide
        )
        held[:, :, lanes] = value.astype(narrow).reshape(held.shape[:2] + (chunk,))
        for j in range(count):
            copies.append(
                pltpu.make_async_copy(
                    held.at[j, :, lanes],
                    out_ref.at[place_ref[4 + first + j], :, lanes],
                    sems.at[j, c],
                )
            )
            copies[-1].start()
    for copy in copies:
        copy.wait()


def back(place, projector, blocks, first, out):
    count = len(blocks)
    cols = blocks[0].shape[0]
    width = projector.shape[0]
    before = [] if out is None else [out]
    return pl.pallas_call(
        functools.partial(back_kernel, count, first),
        out_shape=jax.ShapeDtypeStruct((YHI * X, cols, width), narrow),
        in_specs=[SMEM] + [VMEM] * (1 + count) + [pl.BlockSpec(memory_space=pl.ANY)] * len(before),
        out_specs=pl.BlockSpec(memory_space=pl.ANY),
        input_output_aliases={} if out is None else {2 + count: 0},
        scratch_shapes=[
            pltpu.VMEM((count, cols, width), narrow),
            pltpu.SemaphoreType.DMA((count, CHUNKS)),
        ],
        compiler_params=pltpu.CompilerParams(vmem_limit_bytes=16 * 2**20),
    )(place, projector, *blocks, *before)


def gathered(value, other=None):
    other = swap(value, "yhi") if other is None else other
    mine = [shift(value, "x", X, step) for step in (1, 3, 2)]
    rest = [shift(other, "x", X, step) for step in (1, 3)] + [swap(mine[2], "yhi")]
    return [value, other] + mine + rest


def gathered_from(yhi, x):
    mine, other = yhi * X, (1 - yhi) * X
    steps = [(x + X - step) % X for step in (1, 3, 2)]
    return [mine + x, other + x] + [mine + s for s in steps] + [other + s for s in steps]


def shards(activations, projector, out_grad, first_moment, second_moment):
    n_fsdp = YHI * X
    zh, zl, core, ylo, yhi, x = (
        lax.axis_index(a) for a in ("zh", "zl", "core", "ylo", "yhi", "x")
    )
    tokens, rank = activations.shape[0], projector.shape[1]
    cols = first_moment.shape[1]
    block = CORE * cols
    sources = [(x + X - step) % X for step in (0, 1, 3, 2)]
    place = jnp.stack([ylo, zl, zh, core] + gathered_from(yhi, x) + sources)

    partial_value = jnp.dot(activations, projector, preferred_element_type=wide).astype(narrow)
    partial_value, out_grad = lax.optimization_barrier((partial_value, out_grad))
    share = partial_value.reshape(1, X, tokens // X, rank)
    pieces = lax.all_to_all(
        jnp.broadcast_to(share, (YHI,) + share.shape[1:]).reshape((n_fsdp,) + share.shape[2:]),
        FSDP,
        0,
        0,
    )

    grads = local(
        turn_kernel,
        [((ZH, block, tokens), narrow)] * PARTS,
        1,
        scratch_shapes=[pltpu.VMEM((YLO * ZH * ZL * block, tokens), narrow)],
    )(place, out_grad.reshape(tokens, YLO * ZH * ZL * block))
    moved = exchanged(*grads[1:])
    piece = pieces.astype(wide).sum(0).astype(narrow)
    piece = jnp.stack([piece] + exchanged(piece, piece, piece))
    piece, moved[:2] = lax.optimization_barrier((piece, moved[:2]))
    projected = [piece] + [shift(piece, "x", X, step) for step in (1, 3, 2)]
    grads = [g.reshape(ZH, CORE, cols, tokens) for g in [grads[0]] + moved]
    one = (cols, rank)
    part = (cols, rank // 2)
    sent, whole = local(
        send_kernel,
        [((ZH,) + one, narrow), ((PARTS, X, tokens // X, rank), narrow)],
        X + PARTS,
    )(place, *projected, *grads)
    came = swap(sent, "core")
    (mine,) = local(keep_kernel, [((ZH,) + one, wide)], 1 + PARTS)(place, whole, *grads)
    own, up_far, down_far, up, down, up_held, down_held = local(
        split_kernel, [(one, wide)] + [(part, narrow)] * 4 + [(part, wide)] * 2, 2
    )(place, mine, came)
    up_far, down_far = shift(up_far, "zh", ZH, 1), shift(down_far, "zh", ZH, 3)
    up, down = shift(up, "zh", ZH, 1), shift(down, "zh", ZH, 3)
    up_sum, down_sum = pl.pallas_call(
        relay_kernel,
        out_shape=[jax.ShapeDtypeStruct(part, narrow)] * 2,
        in_specs=[VMEM] * 4,
        out_specs=[VMEM] * 2,
        compiler_params=pltpu.CompilerParams(vmem_limit_bytes=16 * 2**20),
    )(up_held, down_held, up_far, down_far)
    up_sum, down_sum = shift(up_sum, "zh", ZH, 1), shift(down_sum, "zh", ZH, 3)
    moment = jax.ShapeDtypeStruct((1,) + one, wide)
    sums = (own, up, down, up_sum, down_sum, first_moment, second_moment)
    direction = pl.pallas_call(
        direction_kernel,
        out_shape=jax.ShapeDtypeStruct(one, narrow),
        in_specs=[VMEM] * 7,
        out_specs=VMEM,
        compiler_params=pltpu.CompilerParams(vmem_limit_bytes=16 * 2**20),
    )(*sums)
    directions = gathered(direction)
    first_new, second_new = pl.pallas_call(
        moments_kernel,
        out_shape=[moment, moment],
        in_specs=[VMEM] * 7,
        out_specs=[VMEM] * 2,
        compiler_params=pltpu.CompilerParams(vmem_limit_bytes=16 * 2**20),
    )(*sums)
    directions[0], first_new, second_new = lax.optimization_barrier(
        (directions[0], first_new, second_new)
    )
    weight_update = back(place, projector, directions[:5], 0, None)
    weight_update = back(place, projector, directions[5:], 5, weight_update)
    return (weight_update, first_new, second_new)


def solution(mesh):
    fine = Mesh(
        mesh.devices.reshape(YLO, ZH, ZL, CORE, YHI, X), DP + FSDP
    )
    in_specs = (
        P(DP, FSDP),
        P(FSDP, None),
        P(DP, FSDP, None),
        P(FSDP, DP, None),
        P(FSDP, DP, None),
    )
    out_specs = (P(None, DP, FSDP), P(FSDP, DP, None), P(FSDP, DP, None))
    return jax.shard_map(shards, mesh=fine, in_specs=in_specs, out_specs=out_specs, check_vma=False)
```

```python
import functools

import jax
import jax.numpy as jnp
from jax import lax
from jax.experimental import pallas as pl
from jax.experimental.pallas import tpu as pltpu
from jax.sharding import Mesh, PartitionSpec as P

bias_first = 1.0 - 0.9**20
bias_second = 1.0 - 0.999**20
epsilon = 1e-08

YLO, ZH, ZL, CORE = 2, 4, 2, 2
PARTS = YLO * ZL
DP = ("ylo", "zh", "zl", "core")
YHI, X = 2, 4
CHUNKS = 2
FSDP = ("yhi", "x")
wide, narrow = jnp.float32, jnp.bfloat16
VMEM = pl.BlockSpec(memory_space=pltpu.VMEM)
SMEM = pl.BlockSpec(memory_space=pltpu.SMEM)


def swap(value, axis):
    return lax.ppermute(value, axis, [(0, 1), (1, 0)])


def shift(value, axis, size, step):
    return lax.ppermute(value, axis, [(i, (i + step) % size) for i in range(size)])


def exchanged(over_y, over_z, over_both):
    both = lax.ppermute(over_both, ("ylo", "zl"), [(i, 3 - i) for i in range(4)])
    return [swap(over_y, "ylo"), swap(over_z, "zl"), both]


def local(body, outs, count, **kwargs):
    return pl.pallas_call(
        body,
        out_shape=[jax.ShapeDtypeStruct(shape, dtype) for shape, dtype in outs],
        in_specs=[SMEM] + [VMEM] * count,
        out_specs=[VMEM] * len(outs),
        compiler_params=pltpu.CompilerParams(vmem_limit_bytes=16 * 2**20),
        **kwargs,
    )


def turn_kernel(place_ref, grads_ref, *refs):
    outs, turned = refs[:PARTS], refs[PARTS]
    turned[...] = grads_ref[...].T
    block = outs[0].shape[1]
    for part in range(PARTS):
        y = lax.rem(place_ref[0] + part % 2, YLO)
        z = lax.rem(place_ref[1] + part // 2, ZL)
        for h in range(ZH):
            start = pl.multiple_of(((y * ZH + h) * ZL + z) * block, 16)
            outs[part][h] = turned[pl.ds(start, block), :]


def product(place_ref, core, grads, whole):
    cols, tokens = grads[0].shape[2:]
    rows = []
    for step in range(ZH):
        h = lax.rem(place_ref[2] + step, ZH)
        rows.append(jnp.concatenate([part[h, core] for part in grads], axis=1))
    total = jnp.dot(
        jnp.concatenate(rows, axis=0),
        whole[...].reshape(PARTS * tokens, whole.shape[-1]),
        preferred_element_type=wide,
    )
    return total.reshape(ZH, cols, -1)


def send_kernel(place_ref, *refs):
    pieces, grads, (out_ref, whole) = refs[:X], refs[X : X + PARTS], refs[X + PARTS :]
    for j, piece in enumerate(pieces):
        whole[:, pl.ds(place_ref[4 + YHI * X + j], 1)] = piece[...][:, None]
    out_ref[...] = product(place_ref, 1 - place_ref[3], grads, whole).astype(narrow)


def keep_kernel(place_ref, whole, *refs):
    grads, out_ref = refs[:PARTS], refs[PARTS]
    out_ref[...] = product(place_ref, place_ref[3], grads, whole)


def total(mine_ref, came_ref, step, half):
    return mine_ref[step, :, half] + came_ref[step, :, half].astype(wide)


def halves_of(mine_ref):
    lanes = mine_ref.shape[-1] // 2
    return slice(0, lanes), slice(lanes, 2 * lanes)


def split_kernel(_, mine_ref, came_ref, up_far_ref, down_far_ref, up_ref, down_ref):
    left, right = halves_of(mine_ref)
    up_far_ref[...] = total(mine_ref, came_ref, 2, left).astype(narrow)
    down_far_ref[...] = total(mine_ref, came_ref, 2, right).astype(narrow)
    up_ref[...] = total(mine_ref, came_ref, 1, right).astype(narrow)
    down_ref[...] = total(mine_ref, came_ref, 3, left).astype(narrow)


def relay_kernel(mine_ref, came_ref, up_ref, down_ref, up_out_ref, down_out_ref):
    left, right = halves_of(mine_ref)
    up_out_ref[...] = (total(mine_ref, came_ref, 1, left) + up_ref[...].astype(wide)).astype(narrow)
    down_sum = total(mine_ref, came_ref, 3, right) + down_ref[...].astype(wide)
    down_out_ref[...] = down_sum.astype(narrow)


def moments(mine_ref, came_ref, up_ref, down_ref, up_sum_ref, down_sum_ref, first_ref, second_ref):
    left = down_ref[...].astype(wide) + up_sum_ref[...].astype(wide)
    right = up_ref[...].astype(wide) + down_sum_ref[...].astype(wide)
    own = total(mine_ref, came_ref, 0, slice(None))
    gradient = own + jnp.concatenate([left, right], axis=1)
    first_new = 0.9 * first_ref[0] + 0.1 * gradient
    second_new = 0.999 * second_ref[0] + 0.001 * gradient * gradient
    return first_new, second_new


def direction_kernel(*refs):
    first_new, second_new = moments(*refs[:8])
    root = jnp.sqrt(second_new / bias_second) + epsilon
    refs[8][...] = (first_new / bias_first / root).astype(narrow)


def moments_kernel(*refs):
    refs[8][0], refs[9][0] = moments(*refs[:8])


def back_kernel(count, first, place_ref, projector_ref, *refs):
    blocks = refs[:count]
    out_ref, held, sems = refs[-3:]
    stacked = jnp.concatenate([block[...] for block in blocks], axis=0)
    chunk = projector_ref.shape[0] // CHUNKS
    copies = []
    for c in range(CHUNKS):
        lanes = pl.ds(c * chunk, chunk)
        value = lax.dot_general(
            stacked, projector_ref[lanes, :], (((1,), (1,)), ((), ())), preferred_element_type=wide
        )
        held[:, :, lanes] = value.astype(narrow).reshape(held.shape[:2] + (chunk,))
        for j in range(count):
            copies.append(
                pltpu.make_async_copy(
                    held.at[j, :, lanes],
                    out_ref.at[place_ref[4 + first + j], :, lanes],
                    sems.at[j, c],
                )
            )
            copies[-1].start()
    for copy in copies:
        copy.wait()


def back(place, projector, blocks, first, out):
    count = len(blocks)
    cols = blocks[0].shape[0]
    width = projector.shape[0]
    before = [] if out is None else [out]
    return pl.pallas_call(
        functools.partial(back_kernel, count, first),
        out_shape=jax.ShapeDtypeStruct((YHI * X, cols, width), narrow),
        in_specs=[SMEM] + [VMEM] * (1 + count) + [pl.BlockSpec(memory_space=pl.ANY)] * len(before),
        out_specs=pl.BlockSpec(memory_space=pl.ANY),
        input_output_aliases={} if out is None else {2 + count: 0},
        scratch_shapes=[
            pltpu.VMEM((count, cols, width), narrow),
            pltpu.SemaphoreType.DMA((count, CHUNKS)),
        ],
        compiler_params=pltpu.CompilerParams(vmem_limit_bytes=16 * 2**20),
    )(place, projector, *blocks, *before)


def gathered(value, other=None):
    other = swap(value, "yhi") if other is None else other
    mine = [shift(value, "x", X, step) for step in (1, 3, 2)]
    rest = [shift(other, "x", X, step) for step in (1, 3)] + [swap(mine[2], "yhi")]
    return [value, other] + mine + rest


def gathered_from(yhi, x):
    mine, other = yhi * X, (1 - yhi) * X
    steps = [(x + X - step) % X for step in (1, 3, 2)]
    return [mine + x, other + x] + [mine + s for s in steps] + [other + s for s in steps]


def shards(activations, projector, out_grad, first_moment, second_moment):
    n_fsdp = YHI * X
    zh, zl, core, ylo, yhi, x = (
        lax.axis_index(a) for a in ("zh", "zl", "core", "ylo", "yhi", "x")
    )
    tokens, rank = activations.shape[0], projector.shape[1]
    cols = first_moment.shape[1]
    block = CORE * cols
    sources = [(x + X - step) % X for step in (0, 1, 3, 2)]
    place = jnp.stack([ylo, zl, zh, core] + gathered_from(yhi, x) + sources)

    partial_value = jnp.dot(activations, projector, preferred_element_type=wide).astype(narrow)
    partial_value, out_grad = lax.optimization_barrier((partial_value, out_grad))
    share = partial_value.reshape(1, X, tokens // X, rank)
    pieces = lax.all_to_all(
        jnp.broadcast_to(share, (YHI,) + share.shape[1:]).reshape((n_fsdp,) + share.shape[2:]),
        FSDP,
        0,
        0,
    )

    grads = local(
        turn_kernel,
        [((ZH, block, tokens), narrow)] * PARTS,
        1,
        scratch_shapes=[pltpu.VMEM((YLO * ZH * ZL * block, tokens), narrow)],
    )(place, out_grad.reshape(tokens, YLO * ZH * ZL * block))
    moved = exchanged(*grads[1:])
    piece = pieces.astype(wide).sum(0).astype(narrow)
    piece = jnp.stack([piece] + exchanged(piece, piece, piece))
    piece, moved[:2] = lax.optimization_barrier((piece, moved[:2]))
    projected = [piece] + [shift(piece, "x", X, step) for step in (1, 3, 2)]
    grads = [g.reshape(ZH, CORE, cols, tokens) for g in [grads[0]] + moved]
    one = (cols, rank)
    part = (cols, rank // 2)
    sent, whole = local(
        send_kernel,
        [((ZH,) + one, narrow), ((PARTS, X, tokens // X, rank), narrow)],
        X + PARTS,
    )(place, *projected, *grads)
    came = swap(sent, "core")
    (mine,) = local(keep_kernel, [((ZH,) + one, wide)], 1 + PARTS)(place, whole, *grads)
    up_far, down_far, up, down = local(split_kernel, [(part, narrow)] * 4, 2)(place, mine, came)
    up_far, down_far = shift(up_far, "zh", ZH, 1), shift(down_far, "zh", ZH, 3)
    up, down = shift(up, "zh", ZH, 1), shift(down, "zh", ZH, 3)
    up_sum, down_sum = pl.pallas_call(
        relay_kernel,
        out_shape=[jax.ShapeDtypeStruct(part, narrow)] * 2,
        in_specs=[VMEM] * 4,
        out_specs=[VMEM] * 2,
        compiler_params=pltpu.CompilerParams(vmem_limit_bytes=16 * 2**20),
    )(mine, came, up_far, down_far)
    up_sum, down_sum = shift(up_sum, "zh", ZH, 1), shift(down_sum, "zh", ZH, 3)
    moment = jax.ShapeDtypeStruct((1,) + one, wide)
    sums = (mine, came, up, down, up_sum, down_sum, first_moment, second_moment)
    direction = pl.pallas_call(
        direction_kernel,
        out_shape=jax.ShapeDtypeStruct(one, narrow),
        in_specs=[VMEM] * 8,
        out_specs=VMEM,
        compiler_params=pltpu.CompilerParams(vmem_limit_bytes=16 * 2**20),
    )(*sums)
    directions = gathered(direction)
    first_new, second_new = pl.pallas_call(
        moments_kernel,
        out_shape=[moment, moment],
        in_specs=[VMEM] * 8,
        out_specs=[VMEM] * 2,
        compiler_params=pltpu.CompilerParams(vmem_limit_bytes=16 * 2**20),
    )(*sums)
    directions[0], first_new, second_new = lax.optimization_barrier(
        (directions[0], first_new, second_new)
    )
    weight_update = back(place, projector, directions[:5], 0, None)
    weight_update = back(place, projector, directions[5:], 5, weight_update)
    return (weight_update, first_new, second_new)


def solution(mesh):
    fine = Mesh(
        mesh.devices.reshape(YLO, ZH, ZL, CORE, YHI, X), DP + FSDP
    )
    in_specs = (
        P(DP, FSDP),
        P(FSDP, None),
        P(DP, FSDP, None),
        P(FSDP, DP, None),
        P(FSDP, DP, None),
    )
    out_specs = (P(None, DP, FSDP), P(FSDP, DP, None), P(FSDP, DP, None))
    return jax.shard_map(shards, mesh=fine, in_specs=in_specs, out_specs=out_specs, check_vma=False)
```
